256 devices in a mesh: dp: 64 (over x, z, core), mp: 4 (over y).
Axes of the slice: x: 4, y: 4, z: 8, core: 2. Of those that a mesh axis runs over, the one named last changes fastest.
Arguments:
- grads: bfloat16 [4096, 14336], P('dp', 'mp'), may hold values from -6 to 6
- second_moment: float32 [4096, 14336], P('dp', 'mp'), may hold values from 0.02 to 4
- owners: int32 [4, 56], P('mp'), may hold values from 0 to 63, as said below
- stats_left: float32 [4, 128, 512, 512], P('mp', 'dp'), as said below
- stats_right: float32 [4, 128, 512, 512], P('mp', 'dp'), as said below
- root_left: bfloat16 [4, 128, 512, 512], P('mp', 'dp'), as said below
- root_right: bfloat16 [4, 128, 512, 512], P('mp', 'dp'), as said below
Outputs:
- direction: bfloat16 [4096, 14336], P('dp', 'mp')
- new_moment: float32 [4096, 14336], P('dp', 'mp')
- new_left: float32 [4, 128, 512, 512], P('mp', 'dp')
- new_right: float32 [4, 128, 512, 512], P('mp', 'dp')
The draws below stay inside these ranges and needn't reach their ends.
Inputs may be any that keep to these rules, and one draw needn't show every extreme that they name: In each row of owners no value appears more than 2 times, and in every row some value appears exactly 2 times. `stats_left`: Symmetric. `stats_right`: Symmetric. `root_left`: Symmetric. `root_right`: Symmetric.
All inputs are finite; a program needn't handle non-finite values.
Results may differ from the reference program's by a relative error of at most 0.0054.
Values may be sent and summed in bfloat16 or wider, within the bound.
No kernel may reach another device: no remote copies, remote signals or barrier semaphores. Data moves between devices by JAX's collectives and lax.ppermute only.
A program may use at most 64 MiB of HBM per device.

```python
import jax
import jax.numpy as jnp
from jax import lax

BS = 512
ROWS = 4096
COLS = 14336
NB = 56
CAP = 2
N_DP = 64
N_MP = 4


def symmetric_draw(key, low, high, spread):
    key_diag, key_off = jax.random.split(key)
    shape = (N_MP, N_DP * CAP, BS)
    diag = jnp.exp(jax.random.uniform(key_diag, shape, jnp.float32, jnp.log(low), jnp.log(high)))
    noise = jax.random.normal(key_off, shape + (BS,), jnp.float32) * (spread / BS ** 0.5)
    sym = (noise + jnp.swapaxes(noise, -1, -2)) * 0.7071
    return sym + diag[..., None] * jnp.eye(BS, dtype=jnp.float32)


def draw_second_moment(key, part):
    key = jax.random.fold_in(key, 31)
    row_pos = jnp.arange(ROWS, dtype=jnp.float32)[:, None] / (ROWS - 1)
    tilt = jnp.exp(-jnp.log(9.0) * row_pos)
    base = jnp.exp(jax.random.uniform(key, (ROWS, COLS), jnp.float32, jnp.log(0.25), jnp.log(4.0)))
    return base * tilt


def draw_owners(key, part):
    key = jax.random.fold_in(key, 11)
    keys = jax.random.split(key, N_MP)

    def one_row(row_key):
        key_first, key_rest, key_order = jax.random.split(row_key, 3)
        first = jax.random.randint(key_first, (), 0, N_DP)
        others = jax.random.permutation(key_rest, (N_DP - 1) * CAP)[:NB - CAP] // CAP
        others = others + (others >= first).astype(others.dtype)
        listing = jnp.concatenate([jnp.full((CAP,), first, dtype=others.dtype), others])
        return listing[jax.random.permutation(key_order, NB)]
    return jax.vmap(one_row)(keys).astype(jnp.int32)


def draw_stats_left(key, part):
    key = jax.random.fold_in(key, 21)
    return symmetric_draw(key, 0.5, 2.0, 0.3)


def draw_stats_right(key, part):
    key = jax.random.fold_in(key, 22)
    return symmetric_draw(key, 0.5, 2.0, 0.3)


def draw_root_left(key, part):
    key = jax.random.fold_in(key, 23)
    return symmetric_draw(key, 0.5, 1.5, 0.4).astype(jnp.bfloat16)


def draw_root_right(key, part):
    key = jax.random.fold_in(key, 24)
    return symmetric_draw(key, 0.5, 1.5, 0.4).astype(jnp.bfloat16)


def block_levels(own_key, extent, shards, least, largest):
    gain = 1.0
    for dim, shards_of in shards:
        draws = jax.random.uniform(jax.random.fold_in(jax.random.fold_in(own_key, 6), dim), (shards_of,), jnp.float32, least / len(shards), largest / len(shards))
        gain = gain * jnp.repeat(jnp.exp(draws), extent[dim] // shards_of).reshape((-1,) + (1,) * (len(extent) - 1 - dim))
    return gain


def bell_draw(key, extent, width, bound, pieces=(), held_as=jnp.bfloat16):
    array = jax.random.normal(key, extent, jnp.float32) * width
    if len(pieces) > 0:
        array = block_levels(key, extent, pieces, -0.22, 0.18) * array
    return jnp.clip(array, min=-bound, max=bound).astype(held_as)


def setup_inputs(seed: int = 0) -> dict:
    seeds = jax.random.split(jax.random.key(seed), 8)
    grads = bell_draw(seeds[0], (ROWS, COLS), 1.0, 6.0, ((0, 64), (1, 4)))
    second_moment = draw_second_moment(jax.random.fold_in(seeds[7], 71), 0)
    owners = draw_owners(jax.random.fold_in(seeds[7], 71), 0)
    stats_left = draw_stats_left(jax.random.fold_in(seeds[7], 71), 0)
    stats_right = draw_stats_right(jax.random.fold_in(seeds[7], 71), 0)
    root_left = draw_root_left(jax.random.fold_in(seeds[7], 71), 0)
    root_right = draw_root_right(jax.random.fold_in(seeds[7], 71), 0)
    return {"grads": grads, "second_moment": second_moment, "owners": owners, "stats_left": stats_left, "stats_right": stats_right, "root_left": root_left, "root_right": root_right}


stat_decay = 0.9
moment_decay = 0.99
adam_epsilon = 1e-08
norm_epsilon = 1e-06

def to_blocks(matrix, col_blocks):
    piece = BS // N_DP
    row_blocks = ROWS // BS
    shaped = matrix.reshape(N_DP, row_blocks, piece, col_blocks, BS).transpose(1, 3, 0, 2, 4)
    return shaped.reshape(row_blocks * col_blocks, BS, BS)

def from_blocks(blocks, col_blocks):
    piece = BS // N_DP
    row_blocks = ROWS // BS
    shaped = blocks.reshape(row_blocks, col_blocks, N_DP, piece, BS).transpose(2, 0, 3, 1, 4)
    return shaped.reshape(ROWS, col_blocks * BS)

def reference(grads, second_moment, owners, stats_left, stats_right, root_left, root_right):
    piece = BS // N_DP
    row_blocks = ROWS // BS
    col_width = COLS // N_MP
    col_blocks = col_width // BS
    slot_total = N_DP * CAP
    coef = (1.0 - stat_decay) / BS
    grad_wide = grads.astype(jnp.float32)
    new_moment = moment_decay * second_moment + (1.0 - moment_decay) * grad_wide * grad_wide
    adam = grad_wide / (jnp.sqrt(new_moment) + adam_epsilon)
    block_ids = jnp.arange(NB, dtype=jnp.int32)
    dir_parts = []
    left_parts = []
    right_parts = []
    for group in range(N_MP):
        columns = slice(group * col_width, (group + 1) * col_width)
        blocks = to_blocks(grads[:, columns], col_blocks)
        squares = (adam[:, columns] * adam[:, columns]).reshape(N_DP, row_blocks, piece, col_blocks, BS)
        block_sq = lax.optimization_barrier(jnp.sum(squares, axis=(0, 2, 4))).reshape(NB)
        owner = owners[group]
        earlier = (owner[:, None] == owner[None, :]) & (block_ids[None, :] < block_ids[:, None])
        slot_of = lax.optimization_barrier(jnp.sum(earlier.astype(jnp.int32), axis=1))
        index = (owner * CAP + slot_of).astype(jnp.int32)
        slot_grads = jnp.zeros((slot_total, BS, BS), jnp.bfloat16).at[index].set(blocks)

        def update_stats(items):
            left, right, grad_block = items
            gram_left = jnp.dot(grad_block, grad_block.T, preferred_element_type=jnp.float32)
            gram_right = jnp.dot(grad_block.T, grad_block, preferred_element_type=jnp.float32)
            return (stat_decay * left + coef * gram_left, stat_decay * right + coef * gram_right)
        upd_left, upd_right = lax.map(update_stats, (stats_left[group], stats_right[group], slot_grads))
        left_parts.append(upd_left)
        right_parts.append(upd_right)

        def precondition(items):
            grad_block, adam_sq, left_root, right_root = items
            applied = jnp.dot(left_root, grad_block, preferred_element_type=jnp.float32).astype(jnp.bfloat16)
            precond = jnp.dot(applied, right_root, preferred_element_type=jnp.float32)
            graft_scale = jnp.sqrt(adam_sq) / jnp.sqrt(jnp.sum(precond * precond) + norm_epsilon)
            return (graft_scale * precond).astype(jnp.bfloat16)
        dirs = lax.map(precondition, (blocks, block_sq, root_left[group][index], root_right[group][index]))
        dir_parts.append(from_blocks(dirs, col_blocks))
    direction = jnp.concatenate(dir_parts, axis=1)
    new_left = jnp.stack(left_parts, axis=0)
    new_right = jnp.stack(right_parts, axis=0)
    return (direction, new_moment, new_left, new_right)
```

```python
import functools

import jax
import jax.numpy as jnp
from jax import lax
from jax.experimental import pallas as pl
from jax.experimental.pallas import tpu as pltpu
from jax.sharding import PartitionSpec as P

stat_decay = 0.9
moment_decay = 0.99
adam_epsilon = 1e-08
norm_epsilon = 1e-06
LANES = 128
VMEM_BYTES = 58 * 1024 * 1024


def route_kernel(piece, tiles, col_blocks, n_blocks, owner_ref, me_ref, grads_hbm, out_ref, where_ref, mine_ref, count, grads_ref, sem):
    fetch = pltpu.make_async_copy(grads_hbm, grads_ref, sem)
    fetch.start()
    owner_count = out_ref.shape[0]
    capacity = mine_ref.shape[0]
    me = me_ref[0]
    for o in range(owner_count):
        count[o] = 0
    for s in range(capacity):
        mine_ref[s] = -1
    for b in range(n_blocks):
        o = owner_ref[0, b]
        s = count[o]
        count[o] = s + 1
        where_ref[0, b] = o
        where_ref[1, b] = s

        @pl.when(o == me)
        def _():
            mine_ref[s] = b

    fetch.wait()
    row_blocks = n_blocks // col_blocks
    for r in range(0, row_blocks, 2):
        for c in range(col_blocks):
            wide = grads_ref[r * piece:(r + 2) * piece, c * tiles * LANES:(c + 1) * tiles * LANES]
            wide = wide.astype(jnp.float32)
            for half in range(2):
                b = (r + half) * col_blocks + c
                o = where_ref[0, b]
                s = where_ref[1, b]
                part = wide[half * piece:(half + 1) * piece].astype(jnp.bfloat16)
                for j in range(tiles):
                    out_ref[o, s * tiles + j] = part[:, j * LANES:(j + 1) * LANES]


def apply_kernel(tiles, mine_ref, sums_ref, arrived_hbm, left_hbm, right_hbm, reply_hbm, slots_hbm,
                 arrived, left, right, reply, slots, tail, in_sems, out_sems):
    capacity, owner_count, _, piece, _ = arrived.shape
    size = left.shape[1]
    loads = []
    for s in range(capacity):
        loads.append((
            pltpu.make_async_copy(arrived_hbm.at[:, pl.ds(s * tiles, tiles)], arrived.at[s], in_sems.at[s, 0]),
            pltpu.make_async_copy(left_hbm.at[s], left.at[s], in_sems.at[s, 1]),
            pltpu.make_async_copy(right_hbm.at[s], right.at[s], in_sems.at[s, 2]),
        ))
    for copies in loads:
        for copy in copies:
            copy.start()
    tail[...] = jnp.broadcast_to(sums_ref[...][None], tail.shape)
    stores = [pltpu.make_async_copy(tail, reply_hbm.at[:, capacity * tiles], out_sems.at[0])]
    stores[-1].start()
    for s in range(capacity):
        loads[s][0].wait()
        cols = [arrived[s, :, j].astype(jnp.float32).reshape(size, LANES) for j in range(tiles)]
        grad = jnp.concatenate(cols, axis=1)
        grad = jnp.where(mine_ref[s] >= 0, grad, 0.0).astype(jnp.bfloat16)
        slots[s] = grad
        stores.append(pltpu.make_async_copy(slots.at[s], slots_hbm.at[s], out_sems.at[1 + s]))
        stores[-1].start()
        loads[s][1].wait()
        applied = jnp.dot(left[s], grad, preferred_element_type=jnp.float32).astype(jnp.bfloat16)
        loads[s][2].wait()
        precond = jnp.dot(applied, right[s], preferred_element_type=jnp.float32)
        total = jnp.sum(precond * precond, keepdims=True)
        unit = precond * (1.0 / jnp.sqrt(total + norm_epsilon))
        for j in range(tiles):
            part = unit[:, j * LANES:(j + 1) * LANES].reshape(owner_count, piece, LANES)
            reply[s, :, j] = part.astype(jnp.bfloat16)
        stores.append(pltpu.make_async_copy(reply.at[s], reply_hbm.at[:, pl.ds(s * tiles, tiles)], out_sems.at[1 + capacity + s]))
        stores[-1].start()
    for copy in stores:
        copy.wait()


def place_kernel(piece, tiles, col_blocks, n_blocks, where_ref, back_ref, out_ref):
    sums = jnp.sum(back_ref[:, back_ref.shape[1] - 1].astype(jnp.float32), axis=0)
    sums = sums + pltpu.roll(sums, LANES // 2, 1)
    root = jnp.sqrt(sums)
    row_blocks = n_blocks // col_blocks
    for r in range(0, row_blocks, 2):
        for c in range(col_blocks):
            found = []
            for half in range(2):
                b = (r + half) * col_blocks + c
                found.append((where_ref[0, b], where_ref[1, b], jnp.broadcast_to(root[:, b:b + 1], (piece, LANES))))
            for j in range(tiles):
                parts = [back_ref[o, s * tiles + j].astype(jnp.float32) * scale for o, s, scale in found]
                both = jnp.concatenate(parts, axis=0).astype(jnp.bfloat16)
                start = (c * tiles + j) * LANES
                out_ref[r * piece:(r + 2) * piece, start:start + LANES] = both


def params():
    return pltpu.CompilerParams(vmem_limit_bytes=VMEM_BYTES)


def per_device(grads, second_moment, owners, stats_left, stats_right, root_left, root_right):
    rows_dev, col_width = grads.shape
    block_size = stats_left.shape[2]
    capacity = stats_left.shape[1]
    col_blocks = col_width // block_size
    owner_count = lax.axis_size("dp")
    piece = block_size // owner_count
    row_blocks = rows_dev // piece
    n_blocks = row_blocks * col_blocks
    tiles = block_size // LANES
    coef = (1.0 - stat_decay) / block_size
    me = lax.axis_index("dp").astype(jnp.int32).reshape(1)
    smem = pl.BlockSpec(memory_space=pltpu.SMEM)
    vmem = pl.BlockSpec(memory_space=pltpu.VMEM)
    hbm = pl.BlockSpec(memory_space=pl.ANY)

    outgoing, where, mine = pl.pallas_call(
        functools.partial(route_kernel, piece, tiles, col_blocks, n_blocks),
        out_shape=(
            jax.ShapeDtypeStruct((owner_count, capacity * tiles, piece, LANES), jnp.bfloat16),
            jax.ShapeDtypeStruct((2, n_blocks), jnp.int32),
            jax.ShapeDtypeStruct((capacity,), jnp.int32),
        ),
        in_specs=[smem, smem, hbm],
        out_specs=(vmem, smem, smem),
        scratch_shapes=[
            pltpu.SMEM((owner_count,), jnp.int32),
            pltpu.VMEM((rows_dev, col_width), jnp.bfloat16),
            pltpu.SemaphoreType.DMA(()),
        ],
        compiler_params=params(),
        name="route",
    )(owners, me, grads)
    arrived = lax.all_to_all(outgoing, "dp", split_axis=0, concat_axis=0, tiled=True)

    grad_wide = grads.astype(jnp.float32)
    new_moment = moment_decay * second_moment + (1.0 - moment_decay) * grad_wide * grad_wide
    adam = grad_wide / (jnp.sqrt(new_moment) + adam_epsilon)
    block_sq = jnp.sum(
        (adam * adam).reshape(row_blocks, piece, col_blocks, block_size), axis=(1, 3)
    ).reshape(n_blocks)
    high = block_sq.astype(jnp.bfloat16)
    low = (block_sq - high.astype(jnp.float32)).astype(jnp.bfloat16)
    pad = jnp.zeros((LANES // 2 - n_blocks,), jnp.bfloat16)
    sums = jnp.broadcast_to(jnp.concatenate([high, pad, low, pad])[None], (piece, LANES))

    reply, slot_grads = pl.pallas_call(
        functools.partial(apply_kernel, tiles),
        out_shape=(
            jax.ShapeDtypeStruct((owner_count, capacity * tiles + 1, piece, LANES), jnp.bfloat16),
            jax.ShapeDtypeStruct((capacity, block_size, block_size), jnp.bfloat16),
        ),
        in_specs=[smem, vmem, hbm, hbm, hbm],
        out_specs=(hbm, hbm),
        scratch_shapes=[
            pltpu.VMEM((capacity, owner_count, tiles, piece, LANES), jnp.bfloat16),
            pltpu.VMEM((capacity, block_size, block_size), jnp.bfloat16),
            pltpu.VMEM((capacity, block_size, block_size), jnp.bfloat16),
            pltpu.VMEM((capacity, owner_count, tiles, piece, LANES), jnp.bfloat16),
            pltpu.VMEM((capacity, block_size, block_size), jnp.bfloat16),
            pltpu.VMEM((owner_count, piece, LANES), jnp.bfloat16),
            pltpu.SemaphoreType.DMA((capacity, 3)),
            pltpu.SemaphoreType.DMA((1 + 2 * capacity,)),
        ],
        compiler_params=params(),
        name="apply",
    )(mine, sums, arrived, root_left[0], root_right[0])
    returned = lax.all_to_all(reply, "dp", split_axis=0, concat_axis=0, tiled=True)

    gram_left = jnp.einsum("sik,sjk->sij", slot_grads, slot_grads, preferred_element_type=jnp.float32)
    gram_right = jnp.einsum("ski,skj->sij", slot_grads, slot_grads, preferred_element_type=jnp.float32)
    new_left = stat_decay * stats_left[0] + coef * gram_left
    new_right = stat_decay * stats_right[0] + coef * gram_right

    direction = pl.pallas_call(
        functools.partial(place_kernel, piece, tiles, col_blocks, n_blocks),
        out_shape=jax.ShapeDtypeStruct((rows_dev, col_width), jnp.bfloat16),
        in_specs=[smem, vmem],
        out_specs=vmem,
        compiler_params=params(),
        name="place",
    )(where, returned)
    return (direction, new_moment, new_left[None], new_right[None])


def solution(mesh):
    in_specs = (
        P("dp", "mp"),
        P("dp", "mp"),
        P("mp", None),
        P("mp", "dp", None, None),
        P("mp", "dp", None, None),
        P("mp", "dp", None, None),
        P("mp", "dp", None, None),
    )
    out_specs = (P("dp", "mp"), P("dp", "mp"), P("mp", "dp", None, None), P("mp", "dp", None, None))
    return jax.shard_map(
        per_device, mesh=mesh, in_specs=in_specs, out_specs=out_specs, check_vma=False
    )
```

```python
import functools

import jax
import jax.numpy as jnp
from jax import lax
from jax.experimental import pallas as pl
from jax.experimental.pallas import tpu as pltpu
from jax.sharding import PartitionSpec as P

stat_decay = 0.9
moment_decay = 0.99
adam_epsilon = 1e-08
norm_epsilon = 1e-06
LANES = 128
VMEM_BYTES = 12 * 1024 * 1024
VMEM_WHOLE = 58 * 1024 * 1024


def route_kernel(piece, tiles, col_blocks, n_blocks, owner_hbm, grads_hbm, out_ref, where_ref, mine_ref, owner_ref, count, grads_ref, sems):
    listing = pltpu.make_async_copy(owner_hbm, owner_ref, sems.at[0])
    listing.start()
    fetch = pltpu.make_async_copy(grads_hbm, grads_ref, sems.at[1])
    fetch.start()
    owner_count = out_ref.shape[0]
    capacity = mine_ref.shape[0]
    me = lax.axis_index("dp")
    for o in range(owner_count):
        count[o] = 0
    for s in range(capacity):
        mine_ref[s] = -1
    listing.wait()
    for b in range(n_blocks):
        o = owner_ref[0, b]
        s = count[o]
        count[o] = s + 1
        where_ref[0, b] = o
        where_ref[1, b] = s

        @pl.when(o == me)
        def _():
            mine_ref[s] = b

    fetch.wait()
    row_blocks = n_blocks // col_blocks
    for r in range(0, row_blocks, 2):
        for c in range(col_blocks):
            wide = grads_ref[r * piece:(r + 2) * piece, c * tiles * LANES:(c + 1) * tiles * LANES]
            wide = wide.astype(jnp.float32)
            for half in range(2):
                b = (r + half) * col_blocks + c
                o = where_ref[0, b]
                s = where_ref[1, b]
                part = wide[half * piece:(half + 1) * piece].astype(jnp.bfloat16)
                for j in range(tiles):
                    out_ref[o, s * tiles + j] = part[:, j * LANES:(j + 1) * LANES]


def apply_kernel(tiles, mine_ref, arrived, left_hbm, right_hbm, reply_hbm, slots, left, right, reply, sems):
    owner_count, _, piece, _ = arrived.shape
    capacity, size, _ = slots.shape
    loads = []
    for s in range(capacity):
        loads.append(pltpu.make_async_copy(left_hbm.at[s], left.at[s], sems.at[0, s]))
        loads.append(pltpu.make_async_copy(right_hbm.at[s], right.at[s], sems.at[1, s]))
    for load in loads:
        load.start()
    def gather(s):
        cols = [arrived[:, s * tiles + j].astype(jnp.float32).reshape(size, LANES) for j in range(tiles)]
        grad = jnp.concatenate(cols, axis=1)
        slots[s] = jnp.where(mine_ref[s] >= 0, grad, 0.0).astype(jnp.bfloat16)

    def first(s):
        return jnp.dot(left[s], slots[s], preferred_element_type=jnp.float32).astype(jnp.bfloat16)

    def second(s, applied):
        return jnp.dot(applied, right[s], preferred_element_type=jnp.float32)

    def send(s, precond):
        total = jnp.sum(precond * precond, keepdims=True)
        unit = precond * (1.0 / jnp.sqrt(total + norm_epsilon))
        for j in range(tiles):
            part = unit[:, j * LANES:(j + 1) * LANES].reshape(owner_count, piece, LANES)
            reply[s, :, j] = part.astype(jnp.bfloat16)
        store = pltpu.make_async_copy(reply.at[s], reply_hbm.at[:, pl.ds(s * tiles, tiles)], sems.at[2, s])
        store.start()
        return store

    stores = []
    gather(0)
    loads[0].wait()
    applied = first(0)
    for s in range(1, capacity):
        gather(s)
    for load in loads[1:]:
        load.wait()
    for s in range(capacity):
        precond = second(s, applied)
        if s + 1 < capacity:
            applied = first(s + 1)
        stores.append(send(s, precond))
    for store in stores:
        store.wait()


def place_kernel(piece, tiles, col_blocks, n_blocks, where_ref, sums_ref, back_ref, out_hbm, out_ref, sems):
    root = jnp.sqrt(sums_ref[...])
    row_blocks = n_blocks // col_blocks
    stores = []
    for r in range(0, row_blocks, 2):
        rows = pl.ds(r * piece, 2 * piece)
        for c in range(col_blocks):
            found = []
            for half in range(2):
                b = (r + half) * col_blocks + c
                found.append((where_ref[0, b], where_ref[1, b], jnp.broadcast_to(root[:, b:b + 1], (piece, LANES))))
            for j in range(tiles):
                parts = [back_ref[o, s * tiles + j].astype(jnp.float32) * scale for o, s, scale in found]
                both = jnp.concatenate(parts, axis=0).astype(jnp.bfloat16)
                start = (c * tiles + j) * LANES
                out_ref[r * piece:(r + 2) * piece, start:start + LANES] = both
        stores.append(pltpu.make_async_copy(out_ref.at[rows], out_hbm.at[rows], sems.at[r // 2]))
        stores[-1].start()
    for store in stores:
        store.wait()


def swap(value, step):
    pairs = [(i, i ^ step) for i in range(lax.axis_size("dp"))]
    return lax.ppermute(value, "dp", pairs)


def params(limit=VMEM_BYTES):
    return pltpu.CompilerParams(vmem_limit_bytes=limit)


def per_device(grads, second_moment, owners, stats_left, stats_right, root_left, root_right):
    rows_dev, col_width = grads.shape
    block_size = stats_left.shape[2]
    capacity = stats_left.shape[1]
    col_blocks = col_width // block_size
    owner_count = lax.axis_size("dp")
    piece = block_size // owner_count
    row_blocks = rows_dev // piece
    n_blocks = row_blocks * col_blocks
    tiles = block_size // LANES
    coef = (1.0 - stat_decay) / block_size
    smem = pl.BlockSpec(memory_space=pltpu.SMEM)
    vmem = pl.BlockSpec(memory_space=pltpu.VMEM)
    hbm = pl.BlockSpec(memory_space=pl.ANY)

    outgoing, where, mine = pl.pallas_call(
        functools.partial(route_kernel, piece, tiles, col_blocks, n_blocks),
        out_shape=(
            jax.ShapeDtypeStruct((owner_count, capacity * tiles, piece, LANES), jnp.bfloat16),
            jax.ShapeDtypeStruct((2, n_blocks), jnp.int32),
            jax.ShapeDtypeStruct((capacity,), jnp.int32),
        ),
        in_specs=[hbm, hbm],
        out_specs=(vmem, smem, smem),
        scratch_shapes=[
            pltpu.SMEM((1, n_blocks), jnp.int32),
            pltpu.SMEM((owner_count,), jnp.int32),
            pltpu.VMEM((rows_dev, col_width), jnp.bfloat16),
            pltpu.SemaphoreType.DMA((2,)),
        ],
        compiler_params=params(VMEM_WHOLE),
        name="route",
    )(owners, grads)
    arrived = lax.all_to_all(outgoing, "dp", split_axis=0, concat_axis=0, tiled=True)

    grad_wide = grads.astype(jnp.float32)
    new_moment = moment_decay * second_moment + (1.0 - moment_decay) * grad_wide * grad_wide
    adam = grad_wide / (jnp.sqrt(new_moment) + adam_epsilon)
    block_sq = jnp.sum(
        (adam * adam).reshape(row_blocks, piece, col_blocks, block_size), axis=(1, 3)
    ).reshape(n_blocks)
    sums = block_sq.reshape(1, n_blocks)
    for step in (1, 16, 32):
        sums = sums + swap(sums, step)
    sums = sums + swap(sums, 2) + swap(sums, 4) + swap(sums, 6)

    arrived, sums = lax.optimization_barrier((arrived, sums))
    reply, slot_grads = pl.pallas_call(
        functools.partial(apply_kernel, tiles),
        out_shape=(
            jax.ShapeDtypeStruct((owner_count, capacity * tiles, piece, LANES), jnp.bfloat16),
            jax.ShapeDtypeStruct((capacity, block_size, block_size), jnp.bfloat16),
        ),
        in_specs=[smem, vmem, hbm, hbm],
        out_specs=(hbm, vmem),
        scratch_shapes=[
            pltpu.VMEM((capacity, block_size, block_size), jnp.bfloat16),
            pltpu.VMEM((capacity, block_size, block_size), jnp.bfloat16),
            pltpu.VMEM((capacity, owner_count, tiles, piece, LANES), jnp.bfloat16),
            pltpu.SemaphoreType.DMA((3, capacity)),
        ],
        compiler_params=params(50 * 1024 * 1024),
        name="apply",
    )(mine, arrived, root_left[0], root_right[0])
    returned = lax.all_to_all(reply, "dp", split_axis=0, concat_axis=0, tiled=True)

    sums, slot_grads = lax.optimization_barrier((sums, slot_grads))
    sums = sums + swap(sums, 8)
    gram_left = jnp.einsum("sik,sjk->sij", slot_grads, slot_grads, preferred_element_type=jnp.float32)
    gram_right = jnp.einsum("ski,skj->sij", slot_grads, slot_grads, preferred_element_type=jnp.float32)
    new_left = stat_decay * stats_left[0] + coef * gram_left
    new_right = stat_decay * stats_right[0] + coef * gram_right

    direction = pl.pallas_call(
        functools.partial(place_kernel, piece, tiles, col_blocks, n_blocks),
        out_shape=jax.ShapeDtypeStruct((rows_dev, col_width), jnp.bfloat16),
        in_specs=[smem, vmem, vmem],
        out_specs=hbm,
        scratch_shapes=[
            pltpu.VMEM((rows_dev, col_width), jnp.bfloat16),
            pltpu.SemaphoreType.DMA((row_blocks // 2,)),
        ],
        compiler_params=params(),
        name="place",
    )(where, sums, returned)
    return (direction, new_moment, new_left[None], new_right[None])


def solution(mesh):
    in_specs = (
        P("dp", "mp"),
        P("dp", "mp"),
        P("mp", None),
        P("mp", "dp", None, None),
        P("mp", "dp", None, None),
        P("mp", "dp", None, None),
        P("mp", "dp", None, None),
    )
    out_specs = (P("dp", "mp"), P("dp", "mp"), P("mp", "dp", None, None), P("mp", "dp", None, None))
    return jax.shard_map(
        per_device, mesh=mesh, in_specs=in_specs, out_specs=out_specs, check_vma=False
    )
```

```python
import functools

import jax
import jax.numpy as jnp
from jax import lax
from jax.experimental import pallas as pl
from jax.experimental.pallas import tpu as pltpu
from jax.sharding import PartitionSpec as P

stat_decay = 0.9
moment_decay = 0.99
adam_epsilon = 1e-08
norm_epsilon = 1e-06
LANES = 128
VMEM_BYTES = 12 * 1024 * 1024
VMEM_WHOLE = 58 * 1024 * 1024


def route_kernel(piece, tiles, col_blocks, n_blocks, owner_hbm, grads_hbm, out_ref, where_ref, mine_ref, owner_ref, count, grads_ref, sems):
    listing = pltpu.make_async_copy(owner_hbm, owner_ref, sems.at[0])
    listing.start()
    fetch = pltpu.make_async_copy(grads_hbm, grads_ref, sems.at[1])
    fetch.start()
    owner_count = out_ref.shape[0]
    capacity = mine_ref.shape[0]
    me = lax.axis_index("dp")
    for o in range(owner_count):
        count[o] = 0
    for s in range(capacity):
        mine_ref[s] = -1
    listing.wait()
    for b in range(n_blocks):
        o = owner_ref[0, b]
        s = count[o]
        count[o] = s + 1
        where_ref[0, b] = o
        where_ref[1, b] = s

        @pl.when(o == me)
        def _():
            mine_ref[s] = b

    fetch.wait()
    row_blocks = n_blocks // col_blocks
    for r in range(0, row_blocks, 2):
        for c in range(col_blocks):
            wide = grads_ref[r * piece:(r + 2) * piece, c * tiles * LANES:(c + 1) * tiles * LANES]
            wide = wide.astype(jnp.float32)
            for half in range(2):
                b = (r + half) * col_blocks + c
                o = where_ref[0, b]
                s = where_ref[1, b]
                part = wide[half * piece:(half + 1) * piece].astype(jnp.bfloat16)
                for j in range(tiles):
                    out_ref[o, s * tiles + j] = part[:, j * LANES:(j + 1) * LANES]


def apply_kernel(tiles, mine_ref, arrived, left, right_hbm, spare_hbm, reply_hbm, slots, right, reply, sems):
    owner_count, _, piece, _ = arrived.shape
    capacity, size, _ = slots.shape
    loads = [pltpu.make_async_copy(right_hbm.at[s], right.at[s], sems.at[0, s]) for s in range(capacity)]
    for load in loads:
        load.start()

    def gather(s):
        cols = [arrived[:, s * tiles + j].astype(jnp.float32).reshape(size, LANES) for j in range(tiles)]
        grad = jnp.concatenate(cols, axis=1)
        slots[s] = jnp.where(mine_ref[s] >= 0, grad, 0.0).astype(jnp.bfloat16)

    def first(s):
        return jnp.dot(left[s], slots[s], preferred_element_type=jnp.float32).astype(jnp.bfloat16)

    def second(s, applied):
        return jnp.dot(applied, right[s], preferred_element_type=jnp.float32)

    def send(s, precond):
        total = jnp.sum(precond * precond, keepdims=True)
        unit = precond * (1.0 / jnp.sqrt(total + norm_epsilon))
        for j in range(tiles):
            part = unit[:, j * LANES:(j + 1) * LANES].reshape(owner_count, piece, LANES)
            reply[s, :, j] = part.astype(jnp.bfloat16)
        store = pltpu.make_async_copy(reply.at[s], reply_hbm.at[:, pl.ds(s * tiles, tiles)], sems.at[1, s])
        store.start()
        return store

    stores = []
    gather(0)
    applied = first(0)
    for s in range(1, capacity):
        gather(s)
    for load in loads:
        load.wait()
    for s in range(capacity):
        precond = second(s, applied)
        if s + 1 < capacity:
            applied = first(s + 1)
        stores.append(send(s, precond))
    for store in stores:
        store.wait()


def place_kernel(piece, tiles, col_blocks, n_blocks, where_ref, sums_ref, back_ref, out_hbm, out_ref, sems):
    root = jnp.sqrt(sums_ref[...])
    row_blocks = n_blocks // col_blocks
    stores = []
    for r in range(0, row_blocks, 2):
        rows = pl.ds(r * piece, 2 * piece)
        for c in range(col_blocks):
            found = []
            for half in range(2):
                b = (r + half) * col_blocks + c
                found.append((where_ref[0, b], where_ref[1, b], jnp.broadcast_to(root[:, b:b + 1], (piece, LANES))))
            for j in range(tiles):
                parts = [back_ref[o, s * tiles + j].astype(jnp.float32) * scale for o, s, scale in found]
                both = jnp.concatenate(parts, axis=0).astype(jnp.bfloat16)
                start = (c * tiles + j) * LANES
                out_ref[r * piece:(r + 2) * piece, start:start + LANES] = both
        stores.append(pltpu.make_async_copy(out_ref.at[rows], out_hbm.at[rows], sems.at[r // 2]))
        stores[-1].start()
    for store in stores:
        store.wait()


def swap(value, step):
    pairs = [(i, i ^ step) for i in range(lax.axis_size("dp"))]
    return lax.ppermute(value, "dp", pairs)


def params(limit=VMEM_BYTES):
    return pltpu.CompilerParams(vmem_limit_bytes=limit)


def per_device(grads, second_moment, owners, stats_left, stats_right, root_left, root_right):
    rows_dev, col_width = grads.shape
    block_size = stats_left.shape[2]
    capacity = stats_left.shape[1]
    col_blocks = col_width // block_size
    owner_count = lax.axis_size("dp")
    piece = block_size // owner_count
    row_blocks = rows_dev // piece
    n_blocks = row_blocks * col_blocks
    tiles = block_size // LANES
    coef = (1.0 - stat_decay) / block_size
    smem = pl.BlockSpec(memory_space=pltpu.SMEM)
    vmem = pl.BlockSpec(memory_space=pltpu.VMEM)
    hbm = pl.BlockSpec(memory_space=pl.ANY)

    outgoing, where, mine = pl.pallas_call(
        functools.partial(route_kernel, piece, tiles, col_blocks, n_blocks),
        out_shape=(
            jax.ShapeDtypeStruct((owner_count, capacity * tiles, piece, LANES), jnp.bfloat16),
            jax.ShapeDtypeStruct((2, n_blocks), jnp.int32),
            jax.ShapeDtypeStruct((capacity,), jnp.int32),
        ),
        in_specs=[hbm, hbm],
        out_specs=(vmem, smem, smem),
        scratch_shapes=[
            pltpu.SMEM((1, n_blocks), jnp.int32),
            pltpu.SMEM((owner_count,), jnp.int32),
            pltpu.VMEM((rows_dev, col_width), jnp.bfloat16),
            pltpu.SemaphoreType.DMA((2,)),
        ],
        compiler_params=params(VMEM_WHOLE),
        name="route",
    )(owners, grads)
    arrived = lax.all_to_all(outgoing, "dp", split_axis=0, concat_axis=0, tiled=True)

    grad_wide = grads.astype(jnp.float32)
    new_moment = moment_decay * second_moment + (1.0 - moment_decay) * grad_wide * grad_wide
    adam = grad_wide / (jnp.sqrt(new_moment) + adam_epsilon)
    block_sq = jnp.sum(
        (adam * adam).reshape(row_blocks, piece, col_blocks, block_size), axis=(1, 3)
    ).reshape(n_blocks)
    sums = block_sq.reshape(1, n_blocks)
    for step in (1, 16, 32):
        sums = sums + swap(sums, step)
    sums = sums + swap(sums, 2) + swap(sums, 4) + swap(sums, 6)

    arrived, sums = lax.optimization_barrier((arrived, sums))
    reply, slot_grads = pl.pallas_call(
        functools.partial(apply_kernel, tiles),
        out_shape=(
            jax.ShapeDtypeStruct((owner_count, capacity * tiles, piece, LANES), jnp.bfloat16),
            jax.ShapeDtypeStruct((capacity, block_size, block_size), jnp.bfloat16),
        ),
        in_specs=[smem, vmem, vmem, hbm, hbm],
        out_specs=(hbm, vmem),
        scratch_shapes=[
            pltpu.VMEM((capacity, block_size, block_size), jnp.bfloat16),
            pltpu.VMEM((capacity, owner_count, tiles, piece, LANES), jnp.bfloat16),
            pltpu.SemaphoreType.DMA((2, capacity)),
        ],
        input_output_aliases={4: 0},
        compiler_params=params(49 * 1024 * 1024),
        name="apply",
    )(mine, arrived, root_left[0], root_right[0], outgoing)
    returned = lax.all_to_all(reply, "dp", split_axis=0, concat_axis=0, tiled=True)

    sums, slot_grads = lax.optimization_barrier((sums, slot_grads))
    sums = sums + swap(sums, 8)
    gram_left = jnp.einsum("sik,sjk->sij", slot_grads, slot_grads, preferred_element_type=jnp.float32)
    gram_right = jnp.einsum("ski,skj->sij", slot_grads, slot_grads, preferred_element_type=jnp.float32)
    new_left = stat_decay * stats_left[0] + coef * gram_left
    new_right = stat_decay * stats_right[0] + coef * gram_right

    direction = pl.pallas_call(
        functools.partial(place_kernel, piece, tiles, col_blocks, n_blocks),
        out_shape=jax.ShapeDtypeStruct((rows_dev, col_width), jnp.bfloat16),
        in_specs=[smem, vmem, vmem],
        out_specs=hbm,
        scratch_shapes=[
            pltpu.VMEM((rows_dev, col_width), jnp.bfloat16),
            pltpu.SemaphoreType.DMA((row_blocks // 2,)),
        ],
        compiler_params=params(),
        name="place",
    )(where, sums, returned)
    return (direction, new_moment, new_left[None], new_right[None])


def solution(mesh):
    in_specs = (
        P("dp", "mp"),
        P("dp", "mp"),
        P("mp", None),
        P("mp", "dp", None, None),
        P("mp", "dp", None, None),
        P("mp", "dp", None, None),
        P("mp", "dp", None, None),
    )
    out_specs = (P("dp", "mp"), P("dp", "mp"), P("mp", "dp", None, None), P("mp", "dp", None, None))
    return jax.shard_map(
        per_device, mesh=mesh, in_specs=in_specs, out_specs=out_specs, check_vma=False
    )
```

```python
import functools

import jax
import jax.numpy as jnp
from jax import lax
from jax.experimental import pallas as pl
from jax.experimental.pallas import tpu as pltpu
from jax.sharding import PartitionSpec as P

stat_decay = 0.9
moment_decay = 0.99
adam_epsilon = 1e-08
norm_epsilon = 1e-06
LANES = 128
VMEM_BYTES = 12 * 1024 * 1024
VMEM_WHOLE = 58 * 1024 * 1024


def route_kernel(piece, tiles, col_blocks, n_blocks, owner_hbm, grads_hbm, out_ref, where_ref, mine_ref, owner_ref, count, grads_ref, sems):
    listing = pltpu.make_async_copy(owner_hbm, owner_ref, sems.at[0])
    listing.start()
    fetch = pltpu.make_async_copy(grads_hbm, grads_ref, sems.at[1])
    fetch.start()
    owner_count = out_ref.shape[0]
    capacity = mine_ref.shape[0]
    me = lax.axis_index("dp")
    for o in range(owner_count):
        count[o] = 0
    for s in range(capacity):
        mine_ref[s] = -1
    listing.wait()
    for b in range(n_blocks):
        o = owner_ref[0, b]
        s = count[o]
        count[o] = s + 1
        where_ref[0, b] = o
        where_ref[1, b] = s

        @pl.when(o == me)
        def _():
            mine_ref[s] = b

    fetch.wait()
    row_blocks = n_blocks // col_blocks
    for r in range(0, row_blocks, 2):
        for c in range(col_blocks):
            wide = grads_ref[r * piece:(r + 2) * piece, c * tiles * LANES:(c + 1) * tiles * LANES]
            wide = wide.astype(jnp.float32)
            for half in range(2):
                b = (r + half) * col_blocks + c
                o = where_ref[0, b]
                s = where_ref[1, b]
                part = wide[half * piece:(half + 1) * piece].astype(jnp.bfloat16)
                for j in range(tiles):
                    out_ref[o, s * tiles + j] = part[:, j * LANES:(j + 1) * LANES]


def apply_kernel(tiles, mine_hbm, arrived, left, right_hbm, spare_hbm, reply_hbm, slots, right, reply, mine_ref, mine_sem, sems):
    owner_count, _, piece, _ = arrived.shape
    capacity, size, _ = slots.shape
    loads = [pltpu.make_async_copy(right_hbm.at[s], right.at[s], sems.at[0, s]) for s in range(capacity)]
    for load in loads:
        load.start()
    listing = pltpu.make_async_copy(mine_hbm, mine_ref, mine_sem)
    listing.start()

    def gather(s):
        cols = [arrived[:, s * tiles + j].astype(jnp.float32).reshape(size, LANES) for j in range(tiles)]
        grad = jnp.concatenate(cols, axis=1)
        slots[s] = grad.astype(jnp.bfloat16)

    def first(s):
        return jnp.dot(left[s], slots[s], preferred_element_type=jnp.float32).astype(jnp.bfloat16)

    def second(s, applied):
        return jnp.dot(applied, right[s], preferred_element_type=jnp.float32)

    def send(s, precond):
        total = jnp.sum(precond * precond, keepdims=True)
        unit = precond * (1.0 / jnp.sqrt(total + norm_epsilon))
        for j in range(tiles):
            part = unit[:, j * LANES:(j + 1) * LANES].reshape(owner_count, piece, LANES)
            reply[s, :, j] = part.astype(jnp.bfloat16)
        store = pltpu.make_async_copy(reply.at[s], reply_hbm.at[:, pl.ds(s * tiles, tiles)], sems.at[1, s])
        store.start()
        return store

    stores = []
    gather(0)
    applied = first(0)
    for s in range(1, capacity):
        gather(s)
    for load in loads:
        load.wait()
    for s in range(capacity):
        precond = second(s, applied)
        if s + 1 < capacity:
            applied = first(s + 1)
        stores.append(send(s, precond))
    listing.wait()
    for s in range(capacity):
        @pl.when(mine_ref[s] < 0)
        def _():
            slots[s] = jnp.zeros(slots.shape[1:], slots.dtype)

    for store in stores:
        store.wait()


def place_kernel(piece, tiles, col_blocks, n_blocks, where_ref, sums_ref, back_ref, out_hbm, out_ref, sems):
    root = jnp.sqrt(sums_ref[...])
    row_blocks = n_blocks // col_blocks
    stores = []
    for r in range(0, row_blocks, 2):
        rows = pl.ds(r * piece, 2 * piece)
        for c in range(col_blocks):
            found = []
            for half in range(2):
                b = (r + half) * col_blocks + c
                found.append((where_ref[0, b], where_ref[1, b], jnp.broadcast_to(root[:, b:b + 1], (piece, LANES))))
            for j in range(tiles):
                parts = [back_ref[o, s * tiles + j].astype(jnp.float32) * scale for o, s, scale in found]
                both = jnp.concatenate(parts, axis=0).astype(jnp.bfloat16)
                start = (c * tiles + j) * LANES
                out_ref[r * piece:(r + 2) * piece, start:start + LANES] = both
        stores.append(pltpu.make_async_copy(out_ref.at[rows], out_hbm.at[rows], sems.at[r // 2]))
        stores[-1].start()
    for store in stores:
        store.wait()


def swap(value, step):
    pairs = [(i, i ^ step) for i in range(lax.axis_size("dp"))]
    return lax.ppermute(value, "dp", pairs)


def params(limit=VMEM_BYTES):
    return pltpu.CompilerParams(vmem_limit_bytes=limit)


def per_device(grads, second_moment, owners, stats_left, stats_right, root_left, root_right):
    rows_dev, col_width = grads.shape
    block_size = stats_left.shape[2]
    capacity = stats_left.shape[1]
    col_blocks = col_width // block_size
    owner_count = lax.axis_size("dp")
    piece = block_size // owner_count
    row_blocks = rows_dev // piece
    n_blocks = row_blocks * col_blocks
    tiles = block_size // LANES
    coef = (1.0 - stat_decay) / block_size
    smem = pl.BlockSpec(memory_space=pltpu.SMEM)
    vmem = pl.BlockSpec(memory_space=pltpu.VMEM)
    hbm = pl.BlockSpec(memory_space=pl.ANY)

    outgoing, where, mine = pl.pallas_call(
        functools.partial(route_kernel, piece, tiles, col_blocks, n_blocks),
        out_shape=(
            jax.ShapeDtypeStruct((owner_count, capacity * tiles, piece, LANES), jnp.bfloat16),
            jax.ShapeDtypeStruct((2, n_blocks), jnp.int32),
            jax.ShapeDtypeStruct((capacity,), jnp.int32),
        ),
        in_specs=[hbm, hbm],
        out_specs=(vmem, smem, smem),
        scratch_shapes=[
            pltpu.SMEM((1, n_blocks), jnp.int32),
            pltpu.SMEM((owner_count,), jnp.int32),
            pltpu.VMEM((rows_dev, col_width), jnp.bfloat16),
            pltpu.SemaphoreType.DMA((2,)),
        ],
        compiler_params=params(VMEM_WHOLE),
        name="route",
    )(owners, grads)
    arrived = lax.all_to_all(outgoing, "dp", split_axis=0, concat_axis=0, tiled=True)

    grad_wide = grads.astype(jnp.float32)
    new_moment = moment_decay * second_moment + (1.0 - moment_decay) * grad_wide * grad_wide
    adam = grad_wide / (jnp.sqrt(new_moment) + adam_epsilon)
    block_sq = jnp.sum(
        (adam * adam).reshape(row_blocks, piece, col_blocks, block_size), axis=(1, 3)
    ).reshape(n_blocks)
    sums = block_sq.reshape(1, n_blocks)
    for step in (1, 16, 32):
        sums = sums + swap(sums, step)
    sums = sums + swap(sums, 2) + swap(sums, 4) + swap(sums, 6)

    arrived, sums = lax.optimization_barrier((arrived, sums))
    reply, slot_grads = pl.pallas_call(
        functools.partial(apply_kernel, tiles),
        out_shape=(
            jax.ShapeDtypeStruct((owner_count, capacity * tiles, piece, LANES), jnp.bfloat16),
            jax.ShapeDtypeStruct((capacity, block_size, block_size), jnp.bfloat16),
        ),
        in_specs=[hbm, vmem, vmem, hbm, hbm],
        out_specs=(hbm, vmem),
        scratch_shapes=[
            pltpu.VMEM((capacity, block_size, block_size), jnp.bfloat16),
            pltpu.VMEM((capacity, owner_count, tiles, piece, LANES), jnp.bfloat16),
            pltpu.SMEM((capacity,), jnp.int32),
            pltpu.SemaphoreType.DMA(()),
            pltpu.SemaphoreType.DMA((2, capacity)),
        ],
        input_output_aliases={4: 0},
        compiler_params=params(49 * 1024 * 1024),
        name="apply",
    )(mine, arrived, root_left[0], root_right[0], outgoing)
    returned = lax.all_to_all(reply, "dp", split_axis=0, concat_axis=0, tiled=True)

    sums, slot_grads = lax.optimization_barrier((sums, slot_grads))
    sums = sums + swap(sums, 8)
    gram_left = jnp.einsum("sik,sjk->sij", slot_grads, slot_grads, preferred_element_type=jnp.float32)
    gram_right = jnp.einsum("ski,skj->sij", slot_grads, slot_grads, preferred_element_type=jnp.float32)
    new_left = stat_decay * stats_left[0] + coef * gram_left
    new_right = stat_decay * stats_right[0] + coef * gram_right

    direction = pl.pallas_call(
        functools.partial(place_kernel, piece, tiles, col_blocks, n_blocks),
        out_shape=jax.ShapeDtypeStruct((rows_dev, col_width), jnp.bfloat16),
        in_specs=[smem, vmem, vmem],
        out_specs=hbm,
        scratch_shapes=[
            pltpu.VMEM((rows_dev, col_width), jnp.bfloat16),
            pltpu.SemaphoreType.DMA((row_blocks // 2,)),
        ],
        compiler_params=params(),
        name="place",
    )(where, sums, returned)
    return (direction, new_moment, new_left[None], new_right[None])


def solution(mesh):
    in_specs = (
        P("dp", "mp"),
        P("dp", "mp"),
        P("mp", None),
        P("mp", "dp", None, None),
        P("mp", "dp", None, None),
        P("mp", "dp", None, None),
        P("mp", "dp", None, None),
    )
    out_specs = (P("dp", "mp"), P("dp", "mp"), P("mp", "dp", None, None), P("mp", "dp", None, None))
    return jax.shard_map(
        per_device, mesh=mesh, in_specs=in_specs, out_specs=out_specs, check_vma=False
    )
```

```python
import functools

import jax
import jax.numpy as jnp
from jax import lax
from jax.experimental import pallas as pl
from jax.experimental.pallas import tpu as pltpu
from jax.sharding import PartitionSpec as P

stat_decay = 0.9
moment_decay = 0.99
adam_epsilon = 1e-08
norm_epsilon = 1e-06
LANES = 128
VMEM_BYTES = 12 * 1024 * 1024
VMEM_WHOLE = 58 * 1024 * 1024


def route_kernel(piece, tiles, col_blocks, n_blocks, owner_hbm, grads_hbm, out_ref, where_ref, mine_ref, owner_ref, count, grads_ref, sems):
    listing = pltpu.make_async_copy(owner_hbm, owner_ref, sems.at[0])
    listing.start()
    fetch = pltpu.make_async_copy(grads_hbm, grads_ref, sems.at[1])
    fetch.start()
    owner_count = out_ref.shape[0]
    capacity = mine_ref.shape[0]
    me = lax.axis_index("dp")
    for o in range(owner_count):
        count[o] = 0
    for s in range(capacity):
        mine_ref[s] = -1
    listing.wait()
    for b in range(n_blocks):
        o = owner_ref[0, b]
        s = count[o]
        count[o] = s + 1
        where_ref[0, b] = o
        where_ref[1, b] = s

        @pl.when(o == me)
        def _():
            mine_ref[s] = b

    fetch.wait()
    row_blocks = n_blocks // col_blocks
    for r in range(0, row_blocks, 2):
        for c in range(col_blocks):
            wide = grads_ref[r * piece:(r + 2) * piece, c * tiles * LANES:(c + 1) * tiles * LANES]
            wide = wide.astype(jnp.float32)
            for half in range(2):
                b = (r + half) * col_blocks + c
                o = where_ref[0, b]
                s = where_ref[1, b]
                part = wide[half * piece:(half + 1) * piece].astype(jnp.bfloat16)
                for j in range(tiles):
                    out_ref[o, s * tiles + j] = part[:, j * LANES:(j + 1) * LANES]


def apply_kernel(tiles, mine_hbm, arrived, left, right_hbm, spare_hbm, reply_hbm, slots, right, reply, mine_ref, mine_sem, sems):
    owner_count, _, piece, _ = arrived.shape
    capacity, size, _ = slots.shape
    loads = [pltpu.make_async_copy(right_hbm.at[s], right.at[s], sems.at[0, s]) for s in range(capacity)]
    for load in loads:
        load.start()
    listing = pltpu.make_async_copy(mine_hbm, mine_ref, mine_sem)
    listing.start()

    def gather(s):
        cols = [arrived[:, s * tiles + j].astype(jnp.float32).reshape(size, LANES) for j in range(tiles)]
        grad = jnp.concatenate(cols, axis=1)
        slots[s] = grad.astype(jnp.bfloat16)

    def first(s):
        return jnp.dot(left[s], slots[s], preferred_element_type=jnp.float32).astype(jnp.bfloat16)

    def second(s, applied):
        return jnp.dot(applied, right[s], preferred_element_type=jnp.float32)

    def send(s, precond):
        total = jnp.sum(precond * precond, keepdims=True)
        unit = precond * (1.0 / jnp.sqrt(total + norm_epsilon))
        for j in range(tiles):
            part = unit[:, j * LANES:(j + 1) * LANES].reshape(owner_count, piece, LANES)
            reply[s, :, j] = part.astype(jnp.bfloat16)
        store = pltpu.make_async_copy(reply.at[s], reply_hbm.at[:, pl.ds(s * tiles, tiles)], sems.at[1, s])
        store.start()
        return store

    stores = []
    gather(0)
    applied = first(0)
    for s in range(1, capacity):
        gather(s)
    for load in loads:
        load.wait()
    for s in range(capacity):
        precond = second(s, applied)
        if s + 1 < capacity:
            applied = first(s + 1)
        stores.append(send(s, precond))
    listing.wait()
    for s in range(capacity):
        @pl.when(mine_ref[s] < 0)
        def _():
            slots[s] = jnp.zeros(slots.shape[1:], slots.dtype)

    for store in stores:
        store.wait()


def place_kernel(piece, tiles, col_blocks, n_blocks, where_ref, sums_ref, back_ref, out_hbm, out_ref, sems):
    root = jnp.sqrt(sums_ref[...])
    row_blocks = n_blocks // col_blocks
    stores = []
    for r in range(0, row_blocks, 2):
        rows = pl.ds(r * piece, 2 * piece)
        for c in range(col_blocks):
            found = []
            for half in range(2):
                b = (r + half) * col_blocks + c
                found.append((where_ref[0, b], where_ref[1, b], jnp.broadcast_to(root[:, b:b + 1], (piece, LANES))))
            for j in range(tiles):
                parts = [back_ref[o, s * tiles + j].astype(jnp.float32) * scale for o, s, scale in found]
                both = jnp.concatenate(parts, axis=0).astype(jnp.bfloat16)
                start = (c * tiles + j) * LANES
                out_ref[r * piece:(r + 2) * piece, start:start + LANES] = both
        stores.append(pltpu.make_async_copy(out_ref.at[rows], out_hbm.at[rows], sems.at[r // 2]))
        stores[-1].start()
    for store in stores:
        store.wait()


def swap(value, step):
    pairs = [(i, i ^ step) for i in range(lax.axis_size("dp"))]
    return lax.ppermute(value, "dp", pairs)


def params(limit=VMEM_BYTES):
    return pltpu.CompilerParams(vmem_limit_bytes=limit)


def per_device(grads, second_moment, owners, stats_left, stats_right, root_left, root_right):
    rows_dev, col_width = grads.shape
    block_size = stats_left.shape[2]
    capacity = stats_left.shape[1]
    col_blocks = col_width // block_size
    owner_count = lax.axis_size("dp")
    piece = block_size // owner_count
    row_blocks = rows_dev // piece
    n_blocks = row_blocks * col_blocks
    tiles = block_size // LANES
    coef = (1.0 - stat_decay) / block_size
    smem = pl.BlockSpec(memory_space=pltpu.SMEM)
    vmem = pl.BlockSpec(memory_space=pltpu.VMEM)
    hbm = pl.BlockSpec(memory_space=pl.ANY)

    outgoing, where, mine = pl.pallas_call(
        functools.partial(route_kernel, piece, tiles, col_blocks, n_blocks),
        out_shape=(
            jax.ShapeDtypeStruct((owner_count, capacity * tiles, piece, LANES), jnp.bfloat16),
            jax.ShapeDtypeStruct((2, n_blocks), jnp.int32),
            jax.ShapeDtypeStruct((capacity,), jnp.int32),
        ),
        in_specs=[hbm, hbm],
        out_specs=(vmem, smem, smem),
        scratch_shapes=[
            pltpu.SMEM((1, n_blocks), jnp.int32),
            pltpu.SMEM((owner_count,), jnp.int32),
            pltpu.VMEM((rows_dev, col_width), jnp.bfloat16),
            pltpu.SemaphoreType.DMA((2,)),
        ],
        compiler_params=params(VMEM_WHOLE),
        name="route",
    )(owners, grads)
    arrived = lax.all_to_all(outgoing, "dp", split_axis=0, concat_axis=0, tiled=True)

    grad_wide = grads.astype(jnp.float32)
    new_moment = moment_decay * second_moment + (1.0 - moment_decay) * grad_wide * grad_wide
    adam = grad_wide / (jnp.sqrt(new_moment) + adam_epsilon)
    block_sq = jnp.sum(
        (adam * adam).reshape(row_blocks, piece, col_blocks, block_size), axis=(1, 3)
    ).reshape(n_blocks)
    sums = block_sq.reshape(1, n_blocks)
    sums = sums + swap(sums, 1)
    sums = sums + swap(sums, 16) + swap(sums, 32) + swap(sums, 48)
    sums = sums + swap(sums, 2) + swap(sums, 4) + swap(sums, 6)

    arrived, sums = lax.optimization_barrier((arrived, sums))
    reply, slot_grads = pl.pallas_call(
        functools.partial(apply_kernel, tiles),
        out_shape=(
            jax.ShapeDtypeStruct((owner_count, capacity * tiles, piece, LANES), jnp.bfloat16),
            jax.ShapeDtypeStruct((capacity, block_size, block_size), jnp.bfloat16),
        ),
        in_specs=[hbm, vmem, vmem, hbm, hbm],
        out_specs=(hbm, vmem),
        scratch_shapes=[
            pltpu.VMEM((capacity, block_size, block_size), jnp.bfloat16),
            pltpu.VMEM((capacity, owner_count, tiles, piece, LANES), jnp.bfloat16),
            pltpu.SMEM((capacity,), jnp.int32),
            pltpu.SemaphoreType.DMA(()),
            pltpu.SemaphoreType.DMA((2, capacity)),
        ],
        input_output_aliases={4: 0},
        compiler_params=params(49 * 1024 * 1024),
        name="apply",
    )(mine, arrived, root_left[0], root_right[0], outgoing)
    returned = lax.all_to_all(reply, "dp", split_axis=0, concat_axis=0, tiled=True)

    sums, slot_grads = lax.optimization_barrier((sums, slot_grads))
    sums = sums + swap(sums, 8)
    gram_left = jnp.einsum("sik,sjk->sij", slot_grads, slot_grads, preferred_element_type=jnp.float32)
    gram_right = jnp.einsum("ski,skj->sij", slot_grads, slot_grads, preferred_element_type=jnp.float32)
    new_left = stat_decay * stats_left[0] + coef * gram_left
    new_right = stat_decay * stats_right[0] + coef * gram_right

    direction = pl.pallas_call(
        functools.partial(place_kernel, piece, tiles, col_blocks, n_blocks),
        out_shape=jax.ShapeDtypeStruct((rows_dev, col_width), jnp.bfloat16),
        in_specs=[smem, vmem, vmem],
        out_specs=hbm,
        scratch_shapes=[
            pltpu.VMEM((rows_dev, col_width), jnp.bfloat16),
            pltpu.SemaphoreType.DMA((row_blocks // 2,)),
        ],
        compiler_params=params(),
        name="place",
    )(where, sums, returned)
    return (direction, new_moment, new_left[None], new_right[None])


def solution(mesh):
    in_specs = (
        P("dp", "mp"),
        P("dp", "mp"),
        P("mp", None),
        P("mp", "dp", None, None),
        P("mp", "dp", None, None),
        P("mp", "dp", None, None),
        P("mp", "dp", None, None),
    )
    out_specs = (P("dp", "mp"), P("dp", "mp"), P("mp", "dp", None, None), P("mp", "dp", None, None))
    return jax.shard_map(
        per_device, mesh=mesh, in_specs=in_specs, out_specs=out_specs, check_vma=False
    )
```
